32 devices in a mesh: pr: 4 (over z), pc: 8 (over y, x, core).
Axes of the slice: x: 2, y: 2, z: 4, core: 2. Of those that a mesh axis runs over, the one named last changes fastest.
Arguments:
- test_points: bfloat16 [65536, 512], P('pr'), may hold values from -15 to 15
- panel_points: bfloat16 [1024, 512], P('pc'), may hold values from -15 to 15
- factor_rows: float32 [1024, 16384], P('pc', 'pr'), may hold values from -0.046875 to 0.046875
- alpha_below: float32 [16384, 128], P(('pr', 'pc')), may hold values from -6 to 6
- targets: float32 [1024, 128], P('pc'), may hold values from -6 to 6
- inverse_block: float32 [1024, 1024], P('pc'), may hold values from -0.008 to 0.08, as said below
- predictions_in: float32 [65536, 128], P(('pr', 'pc')), may hold values from -6 to 6
Outputs:
- predictions: float32 [65536, 128], P(('pr', 'pc'))
The draws below stay inside these ranges and needn't reach their ends.
Inputs may be any that keep to these rules, and one draw needn't show every extreme that they name: `inverse_block`: lower triangular with a positive diagonal.
All inputs are finite; a program needn't handle non-finite values.
Results may differ from the reference program's by a relative error of at most 0.0003.
Values may be sent and summed in bfloat16 or wider, within the bound.
A program may use at most 128 MiB of HBM per device.

```python
import math
import jax
import jax.numpy as jnp
from jax import lax

D = 512
OUTS = 128
PANEL = 1024
LAYERS = 4
TEST_ROW = 16384
NS = 16384
TEST = 65536
N_PR = 4


def point_cloud(key, count, salt):
    centers = jnp.clip(jax.random.normal(jax.random.fold_in(key, 11), (32, D), jnp.float32), -4.0, 4.0)
    member = jax.random.randint(jax.random.fold_in(key, salt + 1), (count,), 0, 32)
    mixing = jax.random.uniform(jax.random.fold_in(key, salt + 2), (count, 1), jnp.float32, 0.2, 0.85)
    noise = jnp.clip(jax.random.normal(jax.random.fold_in(key, salt + 3), (count, D), jnp.float32), -4.0, 4.0)
    scales = jnp.exp(jax.random.uniform(jax.random.fold_in(key, salt + 4), (count, 1), jnp.float32, math.log(0.5), math.log(2.0)))
    points = scales * (jnp.sqrt(mixing) * centers[member] + jnp.sqrt(1.0 - mixing) * noise)
    return points.astype(jnp.bfloat16)


def draw_test_points(key, part):
    return point_cloud(key, TEST, 100)


def draw_panel_points(key, part):
    return point_cloud(key, PANEL, 200)


def draw_inverse_block(key, part):
    rows = jnp.arange(PANEL)[:, None]
    columns = jnp.arange(PANEL)[None, :]
    diagonal = jnp.exp(jax.random.uniform(jax.random.fold_in(key, 301), (PANEL, 1), jnp.float32, math.log(0.02), math.log(0.08)))
    lower = 0.002 * jnp.clip(jax.random.normal(jax.random.fold_in(key, 302), (PANEL, PANEL), jnp.float32), -4.0, 4.0)
    return jnp.where(rows == columns, diagonal, jnp.where(rows > columns, lower, 0.0)).astype(jnp.float32)


def shard_levels(stream_key, shape, cuts, low, largest):
    gain, own = 1.0, jax.random.fold_in(stream_key, 6)
    for dim, shards_of in cuts:
        draws = jnp.exp(jax.random.uniform(jax.random.fold_in(own, dim), (shards_of,), jnp.float32, low / len(cuts), largest / len(cuts)))
        gain = gain * jnp.repeat(draws, shape[dim] // shards_of).reshape([-1 if axis == dim else 1 for axis in range(len(shape))])
    return gain


def normal_values(stream_key, extent, deviation, reach, cuts=(), dtype=jnp.bfloat16):
    drawn = deviation * jax.random.normal(stream_key, extent, jnp.float32)
    if cuts:
        drawn = drawn * shard_levels(stream_key, extent, cuts, -0.22, 0.18)
    return jnp.clip(drawn, -reach, reach).astype(dtype)


def setup_inputs(seed: int = 0) -> dict:
    arg_keys = jax.random.split(jax.random.key(seed), 8)
    test_points = draw_test_points(jax.random.fold_in(arg_keys[7], 71), 0)
    panel_points = draw_panel_points(jax.random.fold_in(arg_keys[7], 71), 0)
    factor_rows = normal_values(arg_keys[2], (PANEL, NS), NS ** -0.5, 0.046875, ((0, 8), (1, 4)), jnp.float32)
    alpha_below = normal_values(arg_keys[3], (NS, OUTS), 1.0, 6.0, ((0, 32),), jnp.float32)
    targets = normal_values(arg_keys[4], (PANEL, OUTS), 1.0, 6.0, ((0, 8),), jnp.float32)
    inverse_block = draw_inverse_block(jax.random.fold_in(arg_keys[7], 71), 0)
    predictions_in = normal_values(arg_keys[6], (TEST, OUTS), 1.0, 6.0, ((0, 32),), jnp.float32)
    return {"test_points": test_points, "panel_points": panel_points, "factor_rows": factor_rows, "alpha_below": alpha_below, "targets": targets, "inverse_block": inverse_block, "predictions_in": predictions_in}


bias_var = 0.1
weight_var = 2.0

def arc_kernel(panel, test):
    cross = jnp.dot(panel, test.T, preferred_element_type=jnp.float32) / D
    panel_var = jnp.einsum('pd,pd->p', panel, panel, preferred_element_type=jnp.float32) / D
    test_var = jnp.einsum('nd,nd->n', test, test, preferred_element_type=jnp.float32) / D
    kern = bias_var + weight_var * cross
    panel_k = bias_var + weight_var * panel_var
    test_k = bias_var + weight_var * test_var
    for level in range(LAYERS):
        spread = jnp.sqrt(panel_k[:, None] * test_k[None, :])
        cosine = kern / spread
        theta = jnp.arccos(cosine)
        kern = bias_var + weight_var / (2.0 * math.pi) * spread * (jnp.sqrt(1.0 - cosine * cosine) + (math.pi - theta) * cosine)
        panel_k = bias_var + 0.5 * weight_var * panel_k
        test_k = bias_var + 0.5 * weight_var * test_k
    return kern

def reference(test_points, panel_points, factor_rows, alpha_below, targets, inverse_block, predictions_in):
    carried = jnp.dot(factor_rows, alpha_below, precision=lax.Precision.HIGHEST, preferred_element_type=jnp.float32)
    residual = targets - carried
    alpha_panel = jnp.dot(inverse_block.T, residual, precision=lax.Precision.HIGHEST, preferred_element_type=jnp.float32)
    blocks = test_points.reshape(N_PR, TEST_ROW, D)

    def one_block(test_block):
        kern = arc_kernel(panel_points, test_block)
        return lax.dot_general(kern, alpha_panel, (((0,), (0,)), ((), ())), precision=lax.Precision.HIGHEST, preferred_element_type=jnp.float32)
    update = lax.map(one_block, blocks).reshape(TEST, OUTS)
    return predictions_in + update
```

```python
import functools

import jax
import jax.numpy as jnp
from jax import lax
from jax.experimental import pallas as pl
from jax.experimental.pallas import tpu as pltpu
from jax.sharding import PartitionSpec as P

BIAS = 0.1
WEIGHT = 2.0
LAYERS = 4
TINY = 1e-30

Q_FULL = (0.300054727, 0.0153848534, 0.00150124533, 0.00136835552)
Q_THIRD = (0.300093128, 0.0151293296, 0.00200751907, 0.00105867372)
Q_FOURTH = (0.300163349, 0.0145595379, 0.00340029868)


def scales(var0):
    var = [BIAS + WEIGHT * var0]
    for _ in range(LAYERS - 1):
        var.append(BIAS + 0.5 * WEIGHT * var[-1])
    inv = [lax.rsqrt(v) for v in var]
    root = [v * r for v, r in zip(var, inv)]
    out = [inv[0]]
    for l in range(LAYERS - 1):
        out += [inv[l + 1], root[l] * inv[l + 1]]
    return out + [root[LAYERS - 1]]


def bump(w, coef):
    w = jnp.maximum(w, TINY)
    y = w * lax.rsqrt(w)
    q = coef[-1]
    for c in coef[-2::-1]:
        q = q * w + c
    return (w * y) * q


def layers(x, row, col, half_width):
    c = (x + BIAS * half_width) * (row(0) * col(0))
    j = jnp.maximum(c, 0.0) + bump(1.0 - jnp.abs(c), Q_FULL)
    c = row(1) * col(1) + (row(2) * col(2)) * j
    j = c + bump(1.0 - c, Q_FULL)
    c = row(3) * col(3) + (row(4) * col(4)) * j
    j = c + bump(1.0 - c, Q_THIRD)
    c = row(5) * col(5) + (row(6) * col(6)) * j
    return (c + bump(1.0 - c, Q_FOURTH)) * row(7)


def split(x):
    hi = x.astype(jnp.bfloat16)
    return hi, (x - hi.astype(jnp.float32)).astype(jnp.bfloat16)


def square_sums(x, lanes):
    f = x.astype(jnp.float32)
    hi, lo = split(f * f)
    ones = jnp.ones((x.shape[1], lanes), jnp.bfloat16)
    return jnp.dot(hi, ones, preferred_element_type=jnp.float32) + jnp.dot(
        lo, ones, preferred_element_type=jnp.float32
    )


NT = (((1,), (1,)), ((), ()))


def kern_body(test, panel, rows, g, col, xbuf):
    tile, width = test.shape
    lanes = 128
    for i, v in enumerate(scales(square_sums(test[...], lanes) / width)[:-1]):
        col[i] = v
    chunks = panel.shape[0] // lanes

    def product(k):
        return lax.dot_general(
            test[...], panel[pl.ds(k * lanes, lanes), :], NT, preferred_element_type=jnp.float32
        )

    xbuf[0] = product(0)
    for k in range(chunks):
        if k + 1 < chunks:
            xbuf[(k + 1) % 2] = product(k + 1)
        cut = pl.ds(k * lanes, lanes)

        def row(i):
            return rows[i : i + 1, cut]

        sub = 128
        for s in range(tile // sub):
            at = pl.ds(s * sub, sub)
            g[at, cut] = layers(xbuf[k % 2, at, :], row, lambda i: col[i, at, :], width / WEIGHT)


def kern_call(test, panel, rows):
    points, width = test.shape
    tile = 256
    return pl.pallas_call(
        kern_body,
        grid=(points // tile,),
        in_specs=[
            pl.BlockSpec((tile, width), lambda i: (i, 0)),
            pl.BlockSpec(panel.shape, lambda i: (0, 0)),
            pl.BlockSpec(rows.shape, lambda i: (0, 0)),
        ],
        out_specs=pl.BlockSpec((tile, panel.shape[0]), lambda i: (i, 0)),
        out_shape=jax.ShapeDtypeStruct((points, panel.shape[0]), jnp.float32),
        scratch_shapes=[
            pltpu.VMEM((7, tile, 128), jnp.float32),
            pltpu.VMEM((2, tile, 128), jnp.float32),
        ],
        compiler_params=pltpu.CompilerParams(vmem_limit_bytes=24 * 2**20),
        cost_estimate=pl.CostEstimate(
            flops=80 * points * panel.shape[0], bytes_accessed=4 * points * panel.shape[0], transcendentals=0
        ),
    )(test, panel, rows)


def body(
    test_points, panel_points, factor_rows, alpha_below, targets, inverse_block, predictions_in
):
    exact = dict(precision=lax.Precision.HIGHEST, preferred_element_type=jnp.float32)
    points, width = predictions_in.shape[0], test_points.shape[1]
    test = lax.dynamic_slice_in_dim(test_points, lax.axis_index("pc") * points, points, 0)
    panel = lax.all_gather(panel_points, "pc", axis=0, tiled=True)
    panel_var = jnp.einsum("pd,pd->p", panel, panel, preferred_element_type=jnp.float32) / width
    factors = scales(panel_var)
    factors[0] = factors[0] * (WEIGHT / width)
    for i in (1, 3, 5):
        factors[i] = BIAS * factors[i]
    rows = jnp.stack(factors)
    g = kern_call(test, panel, rows)

    alpha = lax.all_gather(alpha_below, "pc", axis=0, tiled=True)
    carried = lax.psum(jnp.dot(factor_rows, alpha, **exact), "pr")
    part = lax.dot_general(inverse_block, targets - carried, (((0,), (0,)), ((), ())), **exact)
    weights = lax.psum(part, "pc")
    test_var = jnp.einsum("nd,nd->n", test, test, preferred_element_type=jnp.float32) / width
    scale = scales(test_var)[-1]
    update = scale[:, None] * jnp.dot(g, weights, **exact) + BIAS * jnp.sum(weights, axis=0)
    return predictions_in + update


def solution(mesh):
    placed = (
        P("pr", None),
        P("pc", None),
        P("pc", "pr"),
        P(("pr", "pc"), None),
        P("pc", None),
        P("pc", None),
        P(("pr", "pc"), None),
    )
    return jax.shard_map(
        body, mesh=mesh, in_specs=placed, out_specs=P(("pr", "pc"), None), check_vma=False
    )
```

```python
import functools

import jax
import jax.numpy as jnp
from jax import lax
from jax.experimental import pallas as pl
from jax.experimental.pallas import tpu as pltpu
from jax.sharding import PartitionSpec as P

BIAS = 0.1
WEIGHT = 2.0
LAYERS = 4
TINY = 1e-30

Q_FULL = (0.300054727, 0.0153848534, 0.00150124533, 0.00136835552)
Q_THIRD = (0.300093128, 0.0151293296, 0.00200751907, 0.00105867372)
Q_FOURTH = (0.300163349, 0.0145595379, 0.00340029868)


def scales(var0):
    var = [BIAS + WEIGHT * var0]
    for _ in range(LAYERS - 1):
        var.append(BIAS + 0.5 * WEIGHT * var[-1])
    inv = [lax.rsqrt(v) for v in var]
    root = [v * r for v, r in zip(var, inv)]
    out = [inv[0]]
    for l in range(LAYERS - 1):
        out += [inv[l + 1], root[l] * inv[l + 1]]
    return out + [root[LAYERS - 1]]


def bump(w, coef):
    w = jnp.maximum(w, TINY)
    y = w * lax.rsqrt(w)
    q = coef[-1]
    for c in coef[-2::-1]:
        q = q * w + c
    return (w * y) * q


def layers(x, row, col, half_width):
    c = (x + BIAS * half_width) * (row(0) * col(0))
    j = jnp.maximum(c, 0.0) + bump(1.0 - jnp.abs(c), Q_FULL)
    c = row(1) * col(1) + (row(2) * col(2)) * j
    j = c + bump(1.0 - c, Q_FULL)
    c = row(3) * col(3) + (row(4) * col(4)) * j
    j = c + bump(1.0 - c, Q_THIRD)
    c = row(5) * col(5) + (row(6) * col(6)) * j
    return (c + bump(1.0 - c, Q_FOURTH)) * row(7)


def split(x):
    hi = x.astype(jnp.bfloat16)
    return hi, (x - hi.astype(jnp.float32)).astype(jnp.bfloat16)


def square_sums(x, lanes):
    f = x.astype(jnp.float32)
    hi, lo = split(f * f)
    ones = jnp.ones((x.shape[1], lanes), jnp.bfloat16)
    return jnp.dot(hi, ones, preferred_element_type=jnp.float32) + jnp.dot(
        lo, ones, preferred_element_type=jnp.float32
    )


NT = (((1,), (1,)), ((), ()))
MESH = pl.DeviceIdType.MESH
LANES = 128
TILE = 256
SUB = 128


def dot(a, b):
    return jnp.dot(a, b, preferred_element_type=jnp.float32)


def split_dot(hi, lo, b):
    b_hi, b_lo = split(b)
    n = b.shape[1]
    both = dot(hi, jnp.concatenate([b_hi, b_lo], axis=1))
    return both[:, :n] + (both[:, n:] + dot(lo, b_hi))


def flipped(j, k):
    bit = 1
    while bit <= k:
        if k & bit:
            j = j + bit * (1 - 2 * ((j // bit) % 2))
        bit *= 2
    return j


def kernel(
    n_pr,
    n_pc,
    test_hbm,
    panel,
    factor,
    below,
    targets,
    inverse,
    pred,
    out,
    test,
    panels,
    belows,
    col,
    rows,
    xa,
    xb,
    g_hi,
    g_lo,
    f_hi,
    f_lo,
    i_hi,
    i_lo,
    z_buf,
    part,
    rs_buf,
    ag_buf,
    load_sem,
    p_send,
    p_recv,
    b_send,
    b_recv,
    z_send,
    z_recv,
    r_send,
    r_recv,
    a_send,
    a_recv,
):
    i, j = lax.axis_index("pr"), lax.axis_index("pc")
    points, outs = pred.shape
    block, width = panel.shape
    depth = below.shape[0]
    peers = [flipped(j, k) for k in range(n_pc)]

    load = pltpu.make_async_copy(
        test_hbm.at[pl.ds(pl.multiple_of(j * points, points), points), :], test, load_sem
    )
    load.start()
    panels[0] = panel[...]
    belows[j] = below[...]

    barrier = pltpu.get_barrier_semaphore()
    for k in range(1, n_pc):
        pl.semaphore_signal(barrier, inc=1, device_id={"pc": peers[k]}, device_id_type=MESH)
    for d in range(1, n_pr):
        pl.semaphore_signal(
            barrier, inc=1, device_id={"pr": lax.rem(i + d, n_pr)}, device_id_type=MESH
        )
    pl.semaphore_wait(barrier, n_pc - 1 + n_pr - 1)

    started = []

    def send(src, dst, sends, recvs, k, to):
        copy = pltpu.make_async_remote_copy(
            src_ref=src,
            dst_ref=dst,
            send_sem=sends.at[k],
            recv_sem=recvs.at[k],
            device_id=to,
            device_id_type=MESH,
        )
        copy.start()
        started.append(copy)

    def arrived(dst, sends, recvs, k, to):
        pltpu.make_async_remote_copy(
            src_ref=dst,
            dst_ref=dst,
            send_sem=sends.at[k],
            recv_sem=recvs.at[k],
            device_id=to,
            device_id_type=MESH,
        ).wait_recv()

    def send_panel(k):
        send(panels.at[0], panels.at[k], p_send, p_recv, k, {"pc": peers[k]})

    def send_below(k):
        send(belows.at[j], belows.at[j], b_send, b_recv, k, {"pc": peers[k]})

    evens = list(range(2, n_pc, 2))
    send_panel(1)
    send_panel(2)
    for k in evens:
        send_below(k)
    for k in evens[1:]:
        send_panel(k)
    send_below(1)

    def take_panel(k):
        if k == 0:
            return
        arrived(panels.at[k], p_send, p_recv, k, {"pc": peers[k]})
        if k % 2 == 0:
            send(panels.at[k], panels.at[k + 1], p_send, p_recv, k + 1, {"pc": peers[1]})

    def take_below(k):
        arrived(belows.at[peers[k]], b_send, b_recv, k, {"pc": peers[k]})
        if k % 2 == 0:
            send(belows.at[peers[k]], belows.at[peers[k]], b_send, b_recv, k + 1, {"pc": peers[1]})

    f_hi[...], f_lo[...] = split(factor[...])
    i_hi[...], i_lo[...] = split(inverse[...].T)
    load.wait()

    def side(t, carry):
        at = pl.ds(pl.multiple_of(t * TILE, TILE), TILE)
        for n, v in enumerate(scales(square_sums(test[at, :], LANES) / width)):
            col[n, at, :] = v
        return carry

    lax.fori_loop(0, points // TILE, side, 0)

    def product(t, k):
        at = pl.ds(pl.multiple_of(t * TILE, TILE), TILE)
        return lax.dot_general(test[at, :], panels[k], NT, preferred_element_type=jnp.float32)

    def chunk(k):
        take_panel(k)
        f = panels[k].astype(jnp.float32)
        hi, lo = split(f * f)
        ones = jnp.ones((8, width), jnp.bfloat16)
        sums = lax.dot_general(ones, hi, NT, preferred_element_type=jnp.float32)
        sums = sums + lax.dot_general(ones, lo, NT, preferred_element_type=jnp.float32)
        for n, v in enumerate(scales(sums / width)):
            rows[n] = v * (WEIGHT / width if n == 0 else BIAS if n in (1, 3, 5) else 1.0)

        def finish(x, t):
            for s in range(TILE // SUB):
                at = pl.ds(pl.multiple_of(t * TILE + s * SUB, SUB), SUB)
                g = layers(
                    x[s * SUB : (s + 1) * SUB, :],
                    lambda n: rows[n, 0:1, :],
                    lambda n: col[n, at, :block],
                    width / WEIGHT,
                )
                hi, lo = split(g)
                g_hi[at, k * block : (k + 1) * block] = hi
                g_lo[at, k * block : (k + 1) * block] = lo

        tiles = points // TILE
        xa[...] = product(0, k)

        def step(n, carry):
            xb[...] = product(2 * n + 1, k)
            finish(xa, 2 * n)
            xa[...] = product(lax.rem(2 * n + 2, tiles), k)
            finish(xb, 2 * n + 1)
            return carry

        lax.fori_loop(0, tiles // 2, step, 0)

    def carried_step():
        total = jnp.zeros((block, outs), jnp.float32)
        for s in range(n_pc):
            cut = slice(s * depth, (s + 1) * depth)
            total = total + split_dot(f_hi[:, cut], f_lo[:, cut], belows[s])
        z_buf[0] = total
        for d in range(1, n_pr):
            send(z_buf.at[0], z_buf.at[d], z_send, z_recv, d, {"pr": lax.rem(i + d, n_pr)})

    def solve_step():
        for d in range(1, n_pr):
            arrived(z_buf.at[d], z_send, z_recv, d, {"pr": lax.rem(i + d, n_pr)})
        carried = z_buf[0]
        for d in range(1, n_pr):
            carried = carried + z_buf[d]
        residual = targets[...] - carried
        whole = split_dot(i_hi[...], i_lo[...], residual)
        for s in range(n_pc):
            part[s] = whole[s * block : (s + 1) * block, :]
        for k in range(1, n_pc):
            send(part.at[peers[k]], rs_buf.at[k], r_send, r_recv, k, {"pc": peers[k]})

    def weights_step():
        alpha = part[j]
        for k in range(1, n_pc):
            arrived(rs_buf.at[k], r_send, r_recv, k, {"pc": peers[k]})
            alpha = alpha + rs_buf[k]
        ag_buf[0] = alpha
        for k in range(1, n_pc):
            send(ag_buf.at[0], ag_buf.at[k], a_send, a_recv, k, {"pc": peers[k]})

    half = n_pc // 2
    for k in range(n_pc):
        if k == half - 1:
            for e in evens:
                take_below(e)
        if k == half:
            for o in range(1, n_pc, 2):
                take_below(o)
            carried_step()
        if k == n_pc - 2:
            solve_step()
        chunk(k)
    weights_step()
    for k in range(1, n_pc):
        arrived(ag_buf.at[k], a_send, a_recv, k, {"pc": peers[k]})

    weights = ag_buf[...].reshape(n_pc * block, outs)
    offset = BIAS * jnp.sum(weights, axis=0, keepdims=True)
    w_hi, w_lo = split(weights)
    w_both = jnp.concatenate([w_hi, w_lo], axis=1)

    def update(t, carry):
        at = pl.ds(pl.multiple_of(t * TILE, TILE), TILE)
        both = dot(g_hi[at, :], w_both)
        total = both[:, :outs] + (both[:, outs:] + dot(g_lo[at, :], w_hi))
        out[at, :] = pred[at, :] + (col[7, at, :outs] * total + offset)
        return carry

    lax.fori_loop(0, points // TILE, update, 0)
    for copy in started:
        copy.wait_send()


def call(mesh, *arrays):
    n_pr, n_pc = mesh.shape["pr"], mesh.shape["pc"]
    test, panel, factor, below, targets, inverse, pred = arrays
    points, outs = pred.shape
    block, width = panel.shape
    full = inverse.shape[1]
    f32, bf16 = jnp.float32, jnp.bfloat16
    vmem = pl.BlockSpec(memory_space=pltpu.VMEM)
    sems = [pltpu.SemaphoreType.DMA((n,)) for n in (n_pc, n_pc, n_pr, n_pc, n_pc) for _ in range(2)]
    return pl.pallas_call(
        functools.partial(kernel, n_pr, n_pc),
        in_specs=[pl.BlockSpec(memory_space=pl.ANY)] + [vmem] * 6,
        out_specs=vmem,
        out_shape=jax.ShapeDtypeStruct((points, outs), f32),
        scratch_shapes=[
            pltpu.VMEM((points, width), bf16),
            pltpu.VMEM((n_pc, block, width), bf16),
            pltpu.VMEM((n_pc,) + below.shape, f32),
            pltpu.VMEM((2 * LAYERS, points, LANES), f32),
            pltpu.VMEM((2 * LAYERS, 8, block), f32),
            pltpu.VMEM((TILE, block), f32),
            pltpu.VMEM((TILE, block), f32),
            pltpu.VMEM((points, full), bf16),
            pltpu.VMEM((points, full), bf16),
            pltpu.VMEM(factor.shape, bf16),
            pltpu.VMEM(factor.shape, bf16),
            pltpu.VMEM((full, block), bf16),
            pltpu.VMEM((full, block), bf16),
            pltpu.VMEM((n_pr, block, outs), f32),
            pltpu.VMEM((n_pc, block, outs), f32),
            pltpu.VMEM((n_pc, block, outs), f32),
            pltpu.VMEM((n_pc, block, outs), f32),
            pltpu.SemaphoreType.DMA,
        ]
        + sems,
        compiler_params=pltpu.CompilerParams(
            collective_id=0, has_side_effects=True, vmem_limit_bytes=48 * 2**20
        ),
        cost_estimate=pl.CostEstimate(
            flops=80 * points * full, bytes_accessed=8 * 2**20, transcendentals=0
        ),
    )(*arrays)


def solution(mesh):
    placed = (
        P("pr", None),
        P("pc", None),
        P("pc", "pr"),
        P(("pr", "pc"), None),
        P("pc", None),
        P("pc", None),
        P(("pr", "pc"), None),
    )
    return jax.shard_map(
        functools.partial(call, mesh), mesh=mesh, in_specs=placed, out_specs=P(("pr", "pc"), None), check_vma=False
    )
```
